512 devices in a mesh: dp: 8 (over x, y_hi), mp: 64 (over y_lo, z, core).
Axes of the slice: x: 4, y: 4 (y_hi: 2, y_lo: 2; y = y_hi * 2 + y_lo), z: 16, core: 2. Of those that a mesh axis runs over, the one named last changes fastest.
Arguments:
- inputs: bfloat16 [2048, 3072], P(('dp', 'mp')), may hold values from -1.5 to 1.5
- gain: float32 [3072], replicated, may hold values from 0.1 to 1.9
- w_in: bfloat16 [3072, 12288], P(None, 'mp'), may hold values from -0.109375 to 0.109375
- w_out: bfloat16 [12288, 3072], P('mp'), may hold values from -0.0546875 to 0.0546875
- cotangent: bfloat16 [2048, 3072], P(('dp', 'mp')), may hold values from -6 to 6
Outputs:
- input_grad: bfloat16 [2048, 3072], P(('dp', 'mp'))
- grad_in: bfloat16 [3072, 12288], P(None, 'mp')
- grad_out: bfloat16 [12288, 3072], P('mp')
The draws below stay inside these ranges and needn't reach their ends.
All inputs are finite; a program needn't handle non-finite values.
Results may differ from the reference program's by a relative error of at most 0.017.
Values may be sent and summed in bfloat16 or wider, within the bound.
No kernel may reach another device: no remote copies, remote signals or barrier semaphores. Data moves between devices by JAX's collectives and lax.ppermute only.
A program may use at most 64 MiB of HBM per device.

```python
import math
import jax
import jax.numpy as jnp
from jax import lax

D = 3072
FF = 12288
TOKENS = 256
ALL_TOKENS = 2048
N_DP = 8


def level_of(stream_key, extent, cuts, smallest, largest):
    loudness, own = 1.0, jax.random.fold_in(stream_key, 6)
    for axis_at, shards_of in cuts:
        heights = jnp.exp(jax.random.uniform(jax.random.fold_in(own, axis_at), (shards_of,), jnp.float32, smallest / len(cuts), largest / len(cuts)))
        loudness = loudness * jnp.repeat(heights, extent[axis_at] // shards_of).reshape([-1 if axis == axis_at else 1 for axis in range(len(extent))])
    return loudness


def bell_draw(stream_key, dims, width, limit, split=(), dtype=jnp.bfloat16):
    drawn = width * jax.random.normal(stream_key, dims, jnp.float32)
    if split:
        drawn = drawn * level_of(stream_key, dims, split, -0.22, 0.18)
    return jnp.clip(drawn, -limit, limit).astype(dtype)


def setup_inputs(seed: int = 0) -> dict:
    splits = jax.random.split(jax.random.key(seed), 6)
    inputs = bell_draw(splits[0], (ALL_TOKENS, D), 0.25, 1.5, ((0, 512),))
    gain = jnp.clip(1.0 + 0.18 * jax.random.normal(splits[1], (D,), jnp.float32), 0.1, 1.9)
    w_in = bell_draw(splits[2], (D, FF), D ** -0.5, 0.109375, ((1, 64),))
    w_out = bell_draw(splits[3], (FF, D), FF ** -0.5, 0.0546875, ((0, 64),))
    cotangent = bell_draw(splits[4], (ALL_TOKENS, D), 1.0, 6.0, ((0, 512),))
    return {"inputs": inputs, "gain": gain, "w_in": w_in, "w_out": w_out, "cotangent": cotangent}


def gelu_value(value):
    slope = math.sqrt(2.0 / math.pi)
    return 0.5 * value * (1.0 + jnp.tanh(slope * (value + 0.044715 * value * value * value)))

def gelu_slope(value):
    slope = math.sqrt(2.0 / math.pi)
    tangent = jnp.tanh(slope * (value + 0.044715 * value * value * value))
    return 0.5 * (1.0 + tangent) + 0.5 * value * (1.0 - tangent * tangent) * slope * (1.0 + 3.0 * 0.044715 * value * value)

def reference(inputs, gain, w_in, w_out, cotangent):
    acc_in = jnp.zeros((D, FF), jnp.float32)
    acc_out = jnp.zeros((FF, D), jnp.float32)
    pieces = []
    contract_last = (((1,), (1,)), ((), ()))
    contract_first = (((0,), (0,)), ((), ()))
    for group in range(N_DP):
        rows_in = inputs[group * TOKENS:(group + 1) * TOKENS]
        rows_grad = cotangent[group * TOKENS:(group + 1) * TOKENS]
        widened = rows_in.astype(jnp.float32)
        row_mean = lax.optimization_barrier(jnp.mean(widened, axis=1, keepdims=True))
        centred = widened - row_mean
        variance = lax.optimization_barrier(jnp.mean(centred * centred, axis=1, keepdims=True))
        inverse = 1.0 / jnp.sqrt(variance + 1e-06)
        normal = centred * inverse
        normed = (normal * gain[None, :]).astype(jnp.bfloat16)
        hidden = jnp.dot(normed, w_in, preferred_element_type=jnp.float32)
        activated = gelu_value(hidden).astype(jnp.bfloat16)
        act_grad = lax.dot_general(rows_grad, w_out, contract_last, preferred_element_type=jnp.float32)
        hidden_grad = (act_grad * gelu_slope(hidden)).astype(jnp.bfloat16)
        part_in = lax.dot_general(normed, hidden_grad, contract_first, preferred_element_type=jnp.float32).astype(jnp.bfloat16)
        part_out = lax.dot_general(activated, rows_grad, contract_first, preferred_element_type=jnp.float32).astype(jnp.bfloat16)
        part_in, part_out = lax.optimization_barrier((part_in, part_out))
        acc_in = acc_in + part_in.astype(jnp.float32)
        acc_out = acc_out + part_out.astype(jnp.float32)
        normed_grad = lax.dot_general(hidden_grad, w_in, contract_last, preferred_element_type=jnp.float32)
        scaled = normed_grad * gain[None, :]
        first_mean = lax.optimization_barrier(jnp.mean(scaled, axis=1, keepdims=True))
        second_mean = lax.optimization_barrier(jnp.mean(scaled * normal, axis=1, keepdims=True))
        result = rows_grad.astype(jnp.float32) + (scaled - first_mean - normal * second_mean) * inverse
        pieces.append(result.astype(jnp.bfloat16))
    input_grad = jnp.concatenate(pieces, axis=0)
    grad_in = (acc_in / N_DP).astype(jnp.bfloat16)
    grad_out = (acc_out / N_DP).astype(jnp.bfloat16)
    return (input_grad, grad_in, grad_out)
```

```python
import math

import jax
import jax.numpy as jnp
from jax import lax
from jax.sharding import Mesh, PartitionSpec as P

AXES = ("x", "yh", "yl", "z", "core")
DP = ("x", "yh")
MP = ("yl", "z", "core")
contract_last = (((1,), (1,)), ((), ()))
contract_first = (((0,), (0,)), ((), ()))
SWAP = [(0, 1), (1, 0)]


def gelu_both(value):
    slope = math.sqrt(2.0 / math.pi)
    tangent = jnp.tanh(slope * (value + 0.044715 * value * value * value))
    gelu = 0.5 * value * (1.0 + tangent)
    derivative = 0.5 * (1.0 + tangent) + 0.5 * value * (1.0 - tangent * tangent) * slope * (
        1.0 + 3.0 * 0.044715 * value * value
    )
    return gelu, derivative


def body(inputs, gain, w_in, w_out, cotangent):
    rows, width = inputs.shape
    hidden_units = w_out.shape[0]
    n_dp = lax.axis_size(DP)
    n_z = lax.axis_size("z")
    widened = inputs.astype(jnp.float32)
    row_mean = jnp.mean(widened, axis=1, keepdims=True)
    centred = widened - row_mean
    variance = jnp.mean(centred * centred, axis=1, keepdims=True)
    inverse = 1.0 / jnp.sqrt(variance + 1e-06)
    normal = centred * inverse
    normed = (normal * gain[None, :]).astype(jnp.bfloat16)

    both = jnp.concatenate([normed, cotangent], axis=1)
    both = lax.all_gather(both, "z", axis=0, tiled=True)
    both = jnp.concatenate([both, lax.ppermute(both, "yl", SWAP)], axis=0)
    both = jnp.concatenate([both, lax.ppermute(both, "core", SWAP)], axis=0)
    normed_all, grad_all = both[:, :width], both[:, width:]

    hidden = jnp.dot(normed_all, w_in, preferred_element_type=jnp.float32)
    gelu, derivative = gelu_both(hidden)
    activated = gelu.astype(jnp.bfloat16)
    act_grad = lax.dot_general(grad_all, w_out, contract_last, preferred_element_type=jnp.float32)
    hidden_grad = (act_grad * derivative).astype(jnp.bfloat16)
    part_in = lax.dot_general(
        hidden_grad, normed_all, contract_first, preferred_element_type=jnp.float32
    ).astype(jnp.bfloat16)
    part_out = lax.dot_general(
        activated, grad_all, contract_first, preferred_element_type=jnp.float32
    ).astype(jnp.bfloat16)
    whole_sum = lax.dot_general(
        hidden_grad, w_in, contract_last, preferred_element_type=jnp.float32
    )

    block = hidden_units // n_dp
    parts = jnp.stack(
        [part_in.reshape(n_dp, block, width), part_out.reshape(n_dp, block, width)], axis=1
    ).reshape(n_dp, 2 * block, width)
    parts = lax.all_to_all(parts, DP, 0, 0, tiled=True)
    mine = (jnp.sum(parts.astype(jnp.float32), axis=0) / n_dp).astype(jnp.bfloat16)
    other = lax.ppermute(mine, "yh", SWAP)
    first = lax.axis_index("yh") == 0
    pair = jnp.stack([jnp.where(first, mine, other), jnp.where(first, other, mine)])
    spread = lax.all_gather(pair, "x", axis=0, tiled=True).reshape(n_dp, 2, block, width)
    grad_in = spread[:, 0].reshape(hidden_units, width).T
    grad_out = spread[:, 1].reshape(hidden_units, width)

    for axis in ("core", "yl"):
        half = whole_sum.shape[0] // 2
        away = lax.ppermute(whole_sum[half:].astype(jnp.bfloat16), axis, SWAP)
        whole_sum = whole_sum[:half] + away.astype(jnp.float32)
    terms = whole_sum.astype(jnp.bfloat16).reshape(n_z, rows, width)
    terms = lax.all_to_all(terms, "z", 0, 0, tiled=True)
    normed_grad = jnp.sum(terms.astype(jnp.float32), axis=0)
    scaled = normed_grad * gain[None, :]
    first_mean = jnp.mean(scaled, axis=1, keepdims=True)
    second_mean = jnp.mean(scaled * normal, axis=1, keepdims=True)
    result = cotangent.astype(jnp.float32) + (scaled - first_mean - normal * second_mean) * inverse
    return (result.astype(jnp.bfloat16), grad_in, grad_out)


def solution(mesh):
    fine = Mesh(mesh.devices.reshape(4, 2, 2, 16, 2), AXES)
    rows, hidden_split = P(DP + MP, None), P(None, MP)
    in_specs = (rows, P(), hidden_split, P(MP, None), rows)
    out_specs = (rows, hidden_split, P(MP, None))
    return jax.shard_map(body, mesh=fine, in_specs=in_specs, out_specs=out_specs, check_vma=False)
```

```python
import math

import jax
import jax.numpy as jnp
from jax import lax
from jax.sharding import Mesh, PartitionSpec as P

AXES = ("x", "yh", "yl", "z", "core")
DP = ("x", "yh")
MP = ("yl", "z", "core")
contract_last = (((1,), (1,)), ((), ()))
contract_first = (((0,), (0,)), ((), ()))
SWAP = [(0, 1), (1, 0)]


def gelu_both(value):
    slope = math.sqrt(2.0 / math.pi)
    tangent = jnp.tanh(slope * (value + 0.044715 * value * value * value))
    gelu = 0.5 * value * (1.0 + tangent)
    derivative = 0.5 * (1.0 + tangent) + 0.5 * value * (1.0 - tangent * tangent) * slope * (
        1.0 + 3.0 * 0.044715 * value * value
    )
    return gelu, derivative


def take(pairs, at):
    return lax.dynamic_index_in_dim(pairs, at, 1, False, allow_negative_indices=False)


def body(inputs, gain, w_in, w_out, cotangent):
    rows, width = inputs.shape
    hidden_units = w_out.shape[0]
    n_dp = lax.axis_size(DP)
    n_z = lax.axis_size("z")
    widened = inputs.astype(jnp.float32)
    row_mean = jnp.mean(widened, axis=1, keepdims=True)
    centred = widened - row_mean
    variance = jnp.mean(centred * centred, axis=1, keepdims=True)
    inverse = 1.0 / jnp.sqrt(variance + 1e-06)
    normal = centred * inverse
    normed = (normal * gain[None, :]).astype(jnp.bfloat16)

    both = jnp.concatenate([normed, cotangent], axis=1)
    both = lax.all_gather(both, "z", axis=0, tiled=True)
    both = jnp.concatenate([both, lax.ppermute(both, "yl", SWAP)], axis=0)
    both = jnp.concatenate([both, lax.ppermute(both, "core", SWAP)], axis=0)
    normed_all, grad_all = both[:, :width], both[:, width:]

    hidden = jnp.dot(normed_all, w_in, preferred_element_type=jnp.float32)
    gelu, derivative = gelu_both(hidden)
    activated = gelu.astype(jnp.bfloat16)
    act_grad = lax.dot_general(grad_all, w_out, contract_last, preferred_element_type=jnp.float32)
    hidden_grad = (act_grad * derivative).astype(jnp.bfloat16)
    part_in = lax.dot_general(
        hidden_grad, normed_all, contract_first, preferred_element_type=jnp.float32
    ).astype(jnp.bfloat16)
    part_out = lax.dot_general(
        activated, grad_all, contract_first, preferred_element_type=jnp.float32
    ).astype(jnp.bfloat16)
    parts = jnp.concatenate([part_in, part_out], axis=0).reshape(n_dp, -1, width)
    parts, hidden_grad = lax.optimization_barrier((parts, hidden_grad))
    parts = lax.all_to_all(parts, DP, 0, 0, tiled=True)

    whole_sum = lax.dot_general(
        hidden_grad, w_in, contract_last, preferred_element_type=jnp.float32
    )
    quarter = whole_sum.shape[0] // 4
    size = quarter // 1
    both_swapped = [(k, k ^ 3) for k in range(4)]
    routes = (("yl", SWAP), ("core", SWAP), (("yl", "core"), both_swapped))
    total = whole_sum[:quarter]
    for k, (axis, pairs) in enumerate(routes, 1):
        away = whole_sum[k * quarter : (k + 1) * quarter].astype(jnp.bfloat16)
        away = [lax.ppermute(away[c : c + size], axis, pairs) for c in range(0, quarter, size)]
        total = total + jnp.concatenate(away).astype(jnp.float32)
    whole_sum = total
    at = lax.axis_index("z").astype(jnp.uint32)
    step, bit_at = 1, 0
    while step < n_z:
        if step == 2:
            parts, _ = lax.optimization_barrier((parts, whole_sum))
            mine = (jnp.sum(parts.astype(jnp.float32), axis=0) / n_dp).astype(jnp.bfloat16)
            spread = jnp.broadcast_to(mine[None], (n_dp, *mine.shape))
            spread, whole_sum = lax.optimization_barrier((spread, whole_sum))
            spread = lax.all_to_all(spread, DP, 0, 0, tiled=True)
        bit = (at >> bit_at) & 1
        pairs = whole_sum.reshape(-1, 2, rows, width)
        send = take(pairs, bit ^ 1).reshape(-1, width)
        keep = take(pairs, bit).reshape(-1, width)
        partners = [(z, z ^ step) for z in range(n_z)]
        away = lax.ppermute(send.astype(jnp.bfloat16), "z", partners)
        whole_sum = keep + away.astype(jnp.float32)
        step, bit_at = 2 * step, bit_at + 1
    normed_grad = whole_sum
    spread = spread.reshape(2, hidden_units, width)
    grad_in = spread[0].T
    grad_out = spread[1]
    scaled = normed_grad * gain[None, :]
    first_mean = jnp.mean(scaled, axis=1, keepdims=True)
    second_mean = jnp.mean(scaled * normal, axis=1, keepdims=True)
    result = cotangent.astype(jnp.float32) + (scaled - first_mean - normal * second_mean) * inverse
    return (result.astype(jnp.bfloat16), grad_in, grad_out)


def solution(mesh):
    fine = Mesh(mesh.devices.reshape(4, 2, 2, 16, 2), AXES)
    rows, hidden_split = P(DP + MP, None), P(None, MP)
    in_specs = (rows, P(), hidden_split, P(MP, None), rows)
    out_specs = (rows, hidden_split, P(MP, None))
    return jax.shard_map(body, mesh=fine, in_specs=in_specs, out_specs=out_specs, check_vma=False)
```

```python
import math

import jax
import jax.numpy as jnp
from jax import lax
from jax.sharding import Mesh, PartitionSpec as P

AXES = ("x", "yh", "yl", "z", "core")
DP = ("x", "yh")
MP = ("yl", "z", "core")
contract_last = (((1,), (1,)), ((), ()))
contract_first = (((0,), (0,)), ((), ()))
SWAP = [(0, 1), (1, 0)]


def gelu_both(value):
    slope = math.sqrt(2.0 / math.pi)
    tangent = jnp.tanh(slope * (value + 0.044715 * value * value * value))
    gelu = 0.5 * value * (1.0 + tangent)
    derivative = 0.5 * (1.0 + tangent) + 0.5 * value * (1.0 - tangent * tangent) * slope * (
        1.0 + 3.0 * 0.044715 * value * value
    )
    return gelu, derivative


STAGES = (("core", 1), ("z", 1), ("yl", 1), ("z", 2), ("z", 4), ("z", 8))


def partner(axis, step):
    return [(at, at ^ step) for at in range(lax.axis_size(axis))]


def stage_order(rows, n_z):
    at = lax.broadcasted_iota(jnp.int32, (4 * n_z * rows, 4 * n_z * rows), 0)
    column = lax.broadcasted_iota(jnp.int32, at.shape, 1)
    old = at % rows
    far = jnp.zeros_like(at)
    block = at.shape[0]
    for axis, step in STAGES:
        block //= 2
        bit = (at // block) % 2
        if axis == "z":
            far = far + bit * step
        else:
            old = old + bit * (n_z * rows * (2 if axis == "core" else 1))
    old = old + (far ^ lax.axis_index("z")) * rows
    return (old == column).astype(jnp.bfloat16)


def body(inputs, gain, w_in, w_out, cotangent):
    rows, width = inputs.shape
    n_dp = lax.axis_size(DP)
    n_z = lax.axis_size("z")
    widened = inputs.astype(jnp.float32)
    row_mean = jnp.mean(widened, axis=1, keepdims=True)
    centred = widened - row_mean
    variance = jnp.mean(centred * centred, axis=1, keepdims=True)
    inverse = 1.0 / jnp.sqrt(variance + 1e-06)
    normal = centred * inverse
    normed = (normal * gain[None, :]).astype(jnp.bfloat16)

    both = jnp.concatenate([normed, cotangent], axis=1)
    both = lax.all_gather(both, "z", axis=0, tiled=True)
    both = jnp.concatenate([both, lax.ppermute(both, "yl", SWAP)], axis=0)
    both = jnp.concatenate([both, lax.ppermute(both, "core", SWAP)], axis=0)
    normed_all, grad_all = both[:, :width], both[:, width:]

    hidden = jnp.dot(normed_all, w_in, preferred_element_type=jnp.float32)
    gelu, derivative = gelu_both(hidden)
    activated = gelu.astype(jnp.bfloat16)
    act_grad = lax.dot_general(grad_all, w_out, contract_last, preferred_element_type=jnp.float32)
    hidden_grad = (act_grad * derivative).astype(jnp.bfloat16)
    order = stage_order(rows, n_z)
    ordered = jnp.dot(order, hidden_grad, preferred_element_type=jnp.float32).astype(jnp.bfloat16)
    half = ordered.shape[0] // 2
    send = lax.dot_general(
        ordered[half:], w_in, contract_last, preferred_element_type=jnp.float32
    ).astype(jnp.bfloat16)

    activated, hidden_grad, send = lax.optimization_barrier((activated, hidden_grad, send))
    part_in = lax.dot_general(
        hidden_grad, normed_all, contract_first, preferred_element_type=jnp.float32
    ).astype(jnp.bfloat16)
    part_out = lax.dot_general(
        activated, grad_all, contract_first, preferred_element_type=jnp.float32
    ).astype(jnp.bfloat16)
    parts = jnp.concatenate([part_in, part_out], axis=0).reshape(n_dp, -1, width)
    parts, ordered = lax.optimization_barrier((parts, ordered))
    parts = lax.all_to_all(parts, DP, 0, 0, tiled=True)

    keep = lax.dot_general(ordered[:half], w_in, contract_last, preferred_element_type=jnp.float32)
    for k, (axis, step) in enumerate(STAGES):
        away = lax.ppermute(send, axis, partner(axis, step))
        half = half // 2
        total = keep + away.astype(jnp.float32)
        if k == 2:
            parts, _ = lax.optimization_barrier((parts, total))
            mine = (jnp.sum(parts.astype(jnp.float32), axis=0) / n_dp).astype(jnp.bfloat16)
            spread = jnp.broadcast_to(mine[None], (n_dp, *mine.shape))
        if k == 2:
            spread, total = lax.optimization_barrier((spread, total))
            spread = lax.all_to_all(spread, DP, 0, 0, tiled=True)
        keep, send = total[:half], total[half:].astype(jnp.bfloat16)
    normed_grad = total
    spread = spread.reshape(2, -1, width)
    grad_in = spread[0].T
    grad_out = spread[1]
    scaled = normed_grad * gain[None, :]
    first_mean = jnp.mean(scaled, axis=1, keepdims=True)
    second_mean = jnp.mean(scaled * normal, axis=1, keepdims=True)
    result = cotangent.astype(jnp.float32) + (scaled - first_mean - normal * second_mean) * inverse
    return (result.astype(jnp.bfloat16), grad_in, grad_out)


def solution(mesh):
    fine = Mesh(mesh.devices.reshape(4, 2, 2, 16, 2), AXES)
    rows, hidden_split = P(DP + MP, None), P(None, MP)
    in_specs = (rows, P(), hidden_split, P(MP, None), rows)
    out_specs = (rows, hidden_split, P(MP, None))
    return jax.shard_map(body, mesh=fine, in_specs=in_specs, out_specs=out_specs, check_vma=False)
```

```python
import math

import jax
import jax.numpy as jnp
from jax import lax
from jax.experimental import pallas as pl
from jax.sharding import Mesh, PartitionSpec as P

AXES = ("x", "yh", "yl", "z", "core")
DP = ("x", "yh")
MP = ("yl", "z", "core")
STAGES = (("core", 1, 1), ("z", 1, 1), ("yl", 1, 1), ("z", 2, 1), ("z", 4, 1), ("z", 8, 1))
contract_last = (((1,), (1,)), ((), ()))
contract_first = (((0,), (0,)), ((), ()))


def gelu_both(value):
    slope = math.sqrt(2.0 / math.pi)
    tangent = jnp.tanh(slope * (value + 0.044715 * value * value * value))
    gelu = 0.5 * value * (1.0 + tangent)
    derivative = 0.5 * (1.0 + tangent) + 0.5 * value * (1.0 - tangent * tangent) * slope * (
        1.0 + 3.0 * 0.044715 * value * value
    )
    return gelu, derivative


def swap(rows, axis, step, pieces):
    pairs = [(at, at ^ step) for at in range(lax.axis_size(axis))]
    size = rows.shape[0] // pieces
    moved = [lax.ppermute(rows[k : k + size], axis, pairs) for k in range(0, rows.shape[0], size)]
    return moved


def stage_order(rows, n_z, zero):
    at = lax.broadcasted_iota(jnp.int32, (4 * n_z * rows, 4 * n_z * rows), 0) + zero
    column = lax.broadcasted_iota(jnp.int32, at.shape, 1)
    old = at % rows
    far = jnp.zeros_like(at)
    block = at.shape[0]
    for axis, step, _ in STAGES:
        block //= 2
        bit = (at // block) % 2
        if axis == "z":
            far = far + bit * step
        else:
            old = old + bit * (n_z * rows * (2 if axis == "core" else 1))
    old = old + (far ^ lax.axis_index("z")) * rows
    return (old == column).astype(jnp.bfloat16)


def norm_kernel(inputs, gain, cotangent, joined, normal_out, inverse_out):
    width = inputs.shape[1]
    widened = inputs[...].astype(jnp.float32)
    centred = widened - jnp.mean(widened, axis=1, keepdims=True)
    variance = jnp.mean(centred * centred, axis=1, keepdims=True)
    inverse = 1.0 / jnp.sqrt(variance + 1e-06)
    normal = centred * inverse
    joined[:, :width] = (normal * gain[...]).astype(jnp.bfloat16)
    joined[:, width:] = cotangent[...]
    normal_out[...] = normal
    inverse_out[...] = jnp.broadcast_to(inverse, inverse_out.shape)


def join_normed(inputs, gain, cotangent):
    rows, width = inputs.shape
    return pl.pallas_call(
        norm_kernel,
        out_shape=(
            jax.ShapeDtypeStruct((rows, 2 * width), jnp.bfloat16),
            jax.ShapeDtypeStruct((rows, width), jnp.float32),
            jax.ShapeDtypeStruct((rows, 128), jnp.float32),
        ),
        name="norm",
    )(inputs, gain[None, :], cotangent)


def back_kernel(keep, away, normal, inverse, gain, cotangent, result):
    normal = normal[...]
    scaled = (keep[...] + away[...].astype(jnp.float32)) * gain[...]
    first_mean = jnp.mean(scaled, axis=1, keepdims=True)
    second_mean = jnp.mean(scaled * normal, axis=1, keepdims=True)
    change = (scaled - first_mean - normal * second_mean) * inverse[:, :1]
    result[...] = (cotangent[...].astype(jnp.float32) + change).astype(jnp.bfloat16)


def body(inputs, gain, w_in, w_out, cotangent):
    rows, width = inputs.shape
    n_dp = lax.axis_size(DP)
    n_z = lax.axis_size("z")
    joined, normal, inverse = join_normed(inputs, gain, cotangent)

    both = lax.all_gather(joined, "z", axis=0, tiled=True)
    both, zero = lax.optimization_barrier((both, jnp.int32(0)))
    order = stage_order(rows, n_z, zero)
    both = jnp.concatenate([both, *swap(both, "yl", 1, 2)], axis=0)
    both, order = lax.optimization_barrier((both, order))
    both = jnp.concatenate([both, *swap(both, "core", 1, 1)], axis=0)
    normed_all, grad_all = both[:, :width], both[:, width:]

    hidden = jnp.dot(normed_all, w_in, preferred_element_type=jnp.float32)
    gelu, derivative = gelu_both(hidden)
    activated = gelu.astype(jnp.bfloat16)
    act_grad = lax.dot_general(grad_all, w_out, contract_last, preferred_element_type=jnp.float32)
    hidden_grad = (act_grad * derivative).astype(jnp.bfloat16)
    ordered = jnp.dot(order, hidden_grad, preferred_element_type=jnp.float32).astype(jnp.bfloat16)
    half = ordered.shape[0] // 2
    send = lax.dot_general(
        ordered[half:], w_in, contract_last, preferred_element_type=jnp.float32
    ).astype(jnp.bfloat16)

    activated, hidden_grad, send = lax.optimization_barrier((activated, hidden_grad, send))
    part_in = lax.dot_general(
        hidden_grad, normed_all, contract_first, preferred_element_type=jnp.float32
    ).astype(jnp.bfloat16)
    part_out = lax.dot_general(
        activated, grad_all, contract_first, preferred_element_type=jnp.float32
    ).astype(jnp.bfloat16)
    parts = jnp.concatenate([part_in, part_out], axis=0).reshape(n_dp, -1, width)
    parts, ordered = lax.optimization_barrier((parts, ordered))
    parts = lax.all_to_all(parts, DP, 0, 0, tiled=True)

    keep = lax.dot_general(ordered[:half], w_in, contract_last, preferred_element_type=jnp.float32)
    for k, (axis, step, pieces) in enumerate(STAGES):
        away = jnp.concatenate(swap(send, axis, step, pieces))
        if k == len(STAGES) - 1:
            break
        half = half // 2
        total = keep + away.astype(jnp.float32)
        if k == 2:
            parts, _ = lax.optimization_barrier((parts, total))
            mine = (jnp.sum(parts.astype(jnp.float32), axis=0) / n_dp).astype(jnp.bfloat16)
            spread = jnp.broadcast_to(mine[None], (n_dp, *mine.shape))
        if k == 2:
            spread, total = lax.optimization_barrier((spread, total))
            spread = lax.all_to_all(spread, DP, 0, 0, tiled=True)
        keep, send = total[:half], total[half:].astype(jnp.bfloat16)
    spread = spread.reshape(2, -1, width)
    grad_in = spread[0].T
    grad_out = spread[1]
    input_grad = pl.pallas_call(
        back_kernel,
        out_shape=jax.ShapeDtypeStruct(inputs.shape, jnp.bfloat16),
        cost_estimate=pl.CostEstimate(flops=0, bytes_accessed=0, transcendentals=0),
        name="norm_back",
    )(keep, away, normal, inverse, gain[None, :], cotangent)
    return (input_grad, grad_in, grad_out)


def solution(mesh):
    fine = Mesh(mesh.devices.reshape(4, 2, 2, 16, 2), AXES)
    rows, hidden_split = P(DP + MP, None), P(None, MP)
    in_specs = (rows, P(), hidden_split, P(MP, None), rows)
    out_specs = (rows, hidden_split, P(MP, None))
    return jax.shard_map(body, mesh=fine, in_specs=in_specs, out_specs=out_specs, check_vma=False)
```

```python
import math

import jax
import jax.numpy as jnp
from jax import lax
from jax.experimental import pallas as pl
from jax.sharding import Mesh, PartitionSpec as P

AXES = ("x", "yh", "yl", "z", "core")
DP = ("x", "yh")
MP = ("yl", "z", "core")
STAGES = (("core", (1,)), ("z", (1, 2,)), ("yl", (1,)), ("z", (4, 8,)))
contract_last = (((1,), (1,)), ((), ()))
contract_first = (((0,), (0,)), ((), ()))


def gelu_both(value):
    slope = math.sqrt(2.0 / math.pi)
    tangent = jnp.tanh(slope * (value + 0.044715 * value * value * value))
    gelu = 0.5 * value * (1.0 + tangent)
    derivative = 0.5 * (1.0 + tangent) + 0.5 * value * (1.0 - tangent * tangent) * slope * (
        1.0 + 3.0 * 0.044715 * value * value
    )
    return gelu, derivative


def swap(rows, axis, step):
    return lax.ppermute(rows, axis, [(at, at ^ step) for at in range(lax.axis_size(axis))])


def stage_order(rows, n_z, zero):
    at = lax.broadcasted_iota(jnp.int32, (4 * n_z * rows, 4 * n_z * rows), 0) + zero
    column = lax.broadcasted_iota(jnp.int32, at.shape, 1)
    old = at % rows
    far = jnp.zeros_like(at)
    block = at.shape[0]
    for axis, bits in STAGES:
        for step in reversed(bits):
            block //= 2
            bit = (at // block) % 2
            if axis == "z":
                far = far + bit * step
            else:
                old = old + bit * (n_z * rows * (2 if axis == "core" else 1))
    old = old + (far ^ lax.axis_index("z")) * rows
    return (old == column).astype(jnp.bfloat16)


def norm_kernel(inputs, gain, cotangent, joined, normal_out, inverse_out):
    width = inputs.shape[1]
    widened = inputs[...].astype(jnp.float32)
    centred = widened - jnp.mean(widened, axis=1, keepdims=True)
    variance = jnp.mean(centred * centred, axis=1, keepdims=True)
    inverse = 1.0 / jnp.sqrt(variance + 1e-06)
    normal = centred * inverse
    joined[:, :width] = (normal * gain[...]).astype(jnp.bfloat16)
    joined[:, width:] = cotangent[...]
    normal_out[...] = normal
    inverse_out[...] = jnp.broadcast_to(inverse, inverse_out.shape)


def join_normed(inputs, gain, cotangent):
    rows, width = inputs.shape
    return pl.pallas_call(
        norm_kernel,
        out_shape=(
            jax.ShapeDtypeStruct((rows, 2 * width), jnp.bfloat16),
            jax.ShapeDtypeStruct((rows, width), jnp.float32),
            jax.ShapeDtypeStruct((rows, 128), jnp.float32),
        ),
        name="norm",
    )(inputs, gain[None, :], cotangent)


def back_kernel(keep, normal, inverse, gain, cotangent, *rest):
    *aways, result = rest
    normal = normal[...]
    terms = keep[...]
    for away in aways:
        terms = terms + away[...].astype(jnp.float32)
    scaled = terms * gain[...]
    first_mean = jnp.mean(scaled, axis=1, keepdims=True)
    second_mean = jnp.mean(scaled * normal, axis=1, keepdims=True)
    change = (scaled - first_mean - normal * second_mean) * inverse[:, :1]
    result[...] = (cotangent[...].astype(jnp.float32) + change).astype(jnp.bfloat16)


def body(inputs, gain, w_in, w_out, cotangent):
    rows, width = inputs.shape
    n_dp = lax.axis_size(DP)
    n_z = lax.axis_size("z")
    joined, normal, inverse = join_normed(inputs, gain, cotangent)

    both = lax.all_gather(joined, "z", axis=0, tiled=True)
    both, zero = lax.optimization_barrier((both, jnp.int32(0)))
    order = stage_order(rows, n_z, zero)
    both = jnp.concatenate([both, swap(both, "yl", 1)], axis=0)
    both, order = lax.optimization_barrier((both, order))
    both = jnp.concatenate([both, swap(both, "core", 1)], axis=0)
    normed_all, grad_all = both[:, :width], both[:, width:]

    hidden = jnp.dot(normed_all, w_in, preferred_element_type=jnp.float32)
    gelu, derivative = gelu_both(hidden)
    activated = gelu.astype(jnp.bfloat16)
    act_grad = lax.dot_general(grad_all, w_out, contract_last, preferred_element_type=jnp.float32)
    hidden_grad = (act_grad * derivative).astype(jnp.bfloat16)
    ordered = jnp.dot(order, hidden_grad, preferred_element_type=jnp.float32).astype(jnp.bfloat16)
    half = ordered.shape[0] // 2
    send = lax.dot_general(
        ordered[half:], w_in, contract_last, preferred_element_type=jnp.float32
    ).astype(jnp.bfloat16)

    activated, hidden_grad, send = lax.optimization_barrier((activated, hidden_grad, send))
    part_in = lax.dot_general(
        hidden_grad, normed_all, contract_first, preferred_element_type=jnp.float32
    ).astype(jnp.bfloat16)
    part_out = lax.dot_general(
        activated, grad_all, contract_first, preferred_element_type=jnp.float32
    ).astype(jnp.bfloat16)
    parts = jnp.concatenate([part_in, part_out], axis=0).reshape(n_dp, -1, width)
    parts, ordered = lax.optimization_barrier((parts, ordered))
    parts = lax.all_to_all(parts, DP, 0, 0, tiled=True)

    keep = lax.dot_general(ordered[:half], w_in, contract_last, preferred_element_type=jnp.float32)
    sends = [send]
    for k, (axis, bits) in enumerate(STAGES):
        steps = (*bits, sum(bits))[: len(sends)]
        aways = [swap(send, axis, step) for send, step in zip(sends, steps)]
        if k == len(STAGES) - 1:
            break
        total = keep + sum(away.astype(jnp.float32) for away in aways)
        if k == 2:
            parts, _ = lax.optimization_barrier((parts, total))
            mine = (jnp.sum(parts.astype(jnp.float32), axis=0) / n_dp).astype(jnp.bfloat16)
            spread = jnp.broadcast_to(mine[None], (n_dp, *mine.shape))
        if k == 2:
            spread, total = lax.optimization_barrier((spread, total))
            spread = lax.all_to_all(spread, DP, 0, 0, tiled=True)
        size = total.shape[0] // 2 ** len(STAGES[k + 1][1])
        keep = total[:size]
        sends = [total[q : q + size].astype(jnp.bfloat16) for q in range(size, total.shape[0], size)]
    spread = spread.reshape(2, -1, width)
    grad_in = spread[0].T
    grad_out = spread[1]
    input_grad = pl.pallas_call(
        back_kernel,
        out_shape=jax.ShapeDtypeStruct(inputs.shape, jnp.bfloat16),
        cost_estimate=pl.CostEstimate(flops=0, bytes_accessed=0, transcendentals=0),
        name="norm_back",
    )(keep, normal, inverse, gain[None, :], cotangent, *aways)
    return (input_grad, grad_in, grad_out)


def solution(mesh):
    fine = Mesh(mesh.devices.reshape(4, 2, 2, 16, 2), AXES)
    rows, hidden_split = P(DP + MP, None), P(None, MP)
    in_specs = (rows, P(), hidden_split, P(MP, None), rows)
    out_specs = (rows, hidden_split, P(MP, None))
    return jax.shard_map(body, mesh=fine, in_specs=in_specs, out_specs=out_specs, check_vma=False)
```

```python
import math

import jax
import jax.numpy as jnp
from jax import lax
from jax.experimental import pallas as pl
from jax.sharding import Mesh, PartitionSpec as P

AXES = ("x", "yh", "yl", "zh", "zl", "core")
DP = ("x", "yh")
Z = ("zh", "zl")
MP = ("yl", *Z, "core")
STAGES = (("core", (1,)), (Z, (1, 2,)), ("yl", (1,)), (Z, (4, 8,)))
contract_last = (((1,), (1,)), ((), ()))
contract_first = (((0,), (0,)), ((), ()))


def gelu_both(value):
    slope = math.sqrt(2.0 / math.pi)
    tangent = jnp.tanh(slope * (value + 0.044715 * value * value * value))
    gelu = 0.5 * value * (1.0 + tangent)
    derivative = 0.5 * (1.0 + tangent) + 0.5 * value * (1.0 - tangent * tangent) * slope * (
        1.0 + 3.0 * 0.044715 * value * value
    )
    return gelu, derivative


def swap(rows, axis, step):
    return lax.ppermute(rows, axis, [(at, at ^ step) for at in range(lax.axis_size(axis))])


def stage_order(rows, n_z, zero):
    at = lax.broadcasted_iota(jnp.int32, (4 * n_z * rows, 4 * n_z * rows), 0) + zero
    column = lax.broadcasted_iota(jnp.int32, at.shape, 1)
    old = at % rows
    far = jnp.zeros_like(at)
    block = at.shape[0]
    for axis, bits in STAGES:
        for step in reversed(bits):
            block //= 2
            bit = (at // block) % 2
            if axis == Z:
                far = far + bit * step
            else:
                old = old + bit * (n_z * rows * (2 if axis == "core" else 1))
    old = old + (far % 2) * (n_z // 2 * rows) + (far // 2 ^ lax.axis_index("zh")) * rows
    return (old == column).astype(jnp.bfloat16)


def normalise(inputs):
    widened = inputs[...].astype(jnp.float32)
    centred = widened - jnp.mean(widened, axis=1, keepdims=True)
    variance = jnp.mean(centred * centred, axis=1, keepdims=True)
    inverse = 1.0 / jnp.sqrt(variance + 1e-06)
    return centred * inverse, inverse


def norm_kernel(inputs, gain, cotangent, joined):
    width = inputs.shape[1]
    normal, _ = normalise(inputs)
    joined[:, :width] = (normal * gain[...]).astype(jnp.bfloat16)
    joined[:, width:] = cotangent[...]


def join_normed(inputs, gain, cotangent):
    rows, width = inputs.shape
    return pl.pallas_call(
        norm_kernel,
        out_shape=jax.ShapeDtypeStruct((rows, 2 * width), jnp.bfloat16),
        name="norm",
    )(inputs, gain[None, :], cotangent)


def back_kernel(keep, inputs, gain, cotangent, *rest):
    *aways, result = rest
    normal, inverse = normalise(inputs)
    terms = keep[...]
    for away in aways:
        terms = terms + away[...].astype(jnp.float32)
    scaled = terms * gain[...]
    first_mean = jnp.mean(scaled, axis=1, keepdims=True)
    second_mean = jnp.mean(scaled * normal, axis=1, keepdims=True)
    change = (scaled - first_mean - normal * second_mean) * inverse
    result[...] = (cotangent[...].astype(jnp.float32) + change).astype(jnp.bfloat16)


def body(inputs, gain, w_in, w_out, cotangent):
    rows, width = inputs.shape
    n_dp = lax.axis_size(DP)
    n_z = lax.axis_size(Z)
    joined = join_normed(inputs, gain, cotangent)

    even = lax.all_gather(joined, "zh", axis=0, tiled=True)
    even, zero = lax.optimization_barrier((even, jnp.int32(0)))
    order = stage_order(rows, n_z, zero)
    odd = swap(even, "zl", 1)
    both = jnp.concatenate([even, odd, swap(even, "yl", 1), swap(odd, "yl", 1)], axis=0)
    both, order = lax.optimization_barrier((both, order))
    both = jnp.concatenate([both, swap(both, "core", 1)], axis=0)
    normed_all, grad_all = both[:, :width], both[:, width:]

    hidden = jnp.dot(normed_all, w_in, preferred_element_type=jnp.float32)
    gelu, derivative = gelu_both(hidden)
    activated = gelu.astype(jnp.bfloat16)
    act_grad = lax.dot_general(grad_all, w_out, contract_last, preferred_element_type=jnp.float32)
    hidden_grad = (act_grad * derivative).astype(jnp.bfloat16)
    ordered = jnp.dot(order, hidden_grad, preferred_element_type=jnp.float32).astype(jnp.bfloat16)
    half = ordered.shape[0] // 2
    send = lax.dot_general(
        ordered[half:], w_in, contract_last, preferred_element_type=jnp.float32
    ).astype(jnp.bfloat16)

    activated, hidden_grad, send = lax.optimization_barrier((activated, hidden_grad, send))
    part_in = lax.dot_general(
        hidden_grad, normed_all, contract_first, preferred_element_type=jnp.float32
    ).astype(jnp.bfloat16)
    part_out = lax.dot_general(
        activated, grad_all, contract_first, preferred_element_type=jnp.float32
    ).astype(jnp.bfloat16)
    parts = jnp.concatenate([part_in, part_out], axis=0).reshape(n_dp, -1, width)
    parts, ordered = lax.optimization_barrier((parts, ordered))
    parts = lax.all_to_all(parts, DP, 0, 0, tiled=True)

    keep = lax.dot_general(ordered[:half], w_in, contract_last, preferred_element_type=jnp.float32)
    sends = [send]
    for k, (axis, bits) in enumerate(STAGES):
        steps = (*bits, sum(bits))[: len(sends)]
        aways = [swap(send, axis, step) for send, step in zip(sends, steps)]
        if k == len(STAGES) - 1:
            break
        total = keep + sum(away.astype(jnp.float32) for away in aways)
        if k == 2:
            parts, _ = lax.optimization_barrier((parts, total))
            mine = (jnp.sum(parts.astype(jnp.float32), axis=0) / n_dp).astype(jnp.bfloat16)
            spread = jnp.broadcast_to(mine[None], (n_dp, *mine.shape))
        if k == 2:
            spread, total = lax.optimization_barrier((spread, total))
            spread = lax.all_to_all(spread, DP, 0, 0, tiled=True)
        size = total.shape[0] // 2 ** len(STAGES[k + 1][1])
        keep = total[:size]
        sends = [total[q : q + size].astype(jnp.bfloat16) for q in range(size, total.shape[0], size)]
    spread = spread.reshape(2, -1, width)
    grad_in = spread[0].T
    grad_out = spread[1]
    input_grad = pl.pallas_call(
        back_kernel,
        out_shape=jax.ShapeDtypeStruct(inputs.shape, jnp.bfloat16),
        cost_estimate=pl.CostEstimate(flops=0, bytes_accessed=0, transcendentals=0),
        name="norm_back",
    )(keep, inputs, gain[None, :], cotangent, *aways)
    return (input_grad, grad_in, grad_out)


def solution(mesh):
    fine = Mesh(mesh.devices.reshape(4, 2, 2, 8, 2, 2), AXES)
    rows, hidden_split = P(DP + MP, None), P(None, MP)
    in_specs = (rows, P(), hidden_split, P(MP, None), rows)
    out_specs = (rows, hidden_split, P(MP, None))
    return jax.shard_map(body, mesh=fine, in_specs=in_specs, out_specs=out_specs, check_vma=False)
```

```python
import math

import jax
import jax.numpy as jnp
from jax import lax
from jax.experimental import pallas as pl
from jax.sharding import Mesh, PartitionSpec as P

AXES = ("x", "yh", "yl", "z", "core")
DP = ("x", "yh")
MP = ("yl", "z", "core")
STAGES = (("core", (1,)), ("z", (1, 2,)), ("yl", (1,)), ("z", (4, 8,)))
contract_last = (((1,), (1,)), ((), ()))
contract_first = (((0,), (0,)), ((), ()))


def gelu_both(value):
    slope = math.sqrt(2.0 / math.pi)
    tangent = jnp.tanh(slope * (value + 0.044715 * value * value * value))
    gelu = 0.5 * value * (1.0 + tangent)
    derivative = 0.5 * (1.0 + tangent) + 0.5 * value * (1.0 - tangent * tangent) * slope * (
        1.0 + 3.0 * 0.044715 * value * value
    )
    return gelu, derivative


def swap(rows, axis, step):
    return lax.ppermute(rows, axis, [(at, at ^ step) for at in range(lax.axis_size(axis))])


def stage_order(rows, n_z, zero):
    at = lax.broadcasted_iota(jnp.int32, (4 * n_z * rows, 4 * n_z * rows), 0) + zero
    column = lax.broadcasted_iota(jnp.int32, at.shape, 1)
    old = at % rows
    far = jnp.zeros_like(at)
    block = at.shape[0]
    for axis, bits in STAGES:
        for step in reversed(bits):
            block //= 2
            bit = (at // block) % 2
            if axis == "z":
                far = far + bit * step
            else:
                old = old + bit * (n_z * rows * (2 if axis == "core" else 1))
    old = old + (far ^ lax.axis_index("z")) * rows
    return (old == column).astype(jnp.bfloat16)


def norm_kernel(inputs, gain, cotangent, joined, normal_out, inverse_out):
    width = inputs.shape[1]
    widened = inputs[...].astype(jnp.float32)
    centred = widened - jnp.mean(widened, axis=1, keepdims=True)
    variance = jnp.mean(centred * centred, axis=1, keepdims=True)
    inverse = 1.0 / jnp.sqrt(variance + 1e-06)
    normal = centred * inverse
    joined[:, :width] = (normal * gain[...]).astype(jnp.bfloat16)
    joined[:, width:] = cotangent[...]
    normal_out[...] = normal
    inverse_out[...] = jnp.broadcast_to(inverse, inverse_out.shape)


def join_normed(inputs, gain, cotangent):
    rows, width = inputs.shape
    return pl.pallas_call(
        norm_kernel,
        out_shape=(
            jax.ShapeDtypeStruct((rows, 2 * width), jnp.bfloat16),
            jax.ShapeDtypeStruct((rows, width), jnp.float32),
            jax.ShapeDtypeStruct((rows, 128), jnp.float32),
        ),
        name="norm",
    )(inputs, gain[None, :], cotangent)


def back_kernel(keep, normal, inverse, gain, cotangent, *rest):
    *aways, result = rest
    normal = normal[...]
    terms = keep[...]
    for away in aways:
        terms = terms + away[...].astype(jnp.float32)
    scaled = terms * gain[...]
    first_mean = jnp.mean(scaled, axis=1, keepdims=True)
    second_mean = jnp.mean(scaled * normal, axis=1, keepdims=True)
    change = (scaled - first_mean - normal * second_mean) * inverse[:, :1]
    result[...] = (cotangent[...].astype(jnp.float32) + change).astype(jnp.bfloat16)


def body(inputs, gain, w_in, w_out, cotangent):
    rows, width = inputs.shape
    n_dp = lax.axis_size(DP)
    n_z = lax.axis_size("z")
    joined, normal, inverse = join_normed(inputs, gain, cotangent)

    both = lax.all_gather(joined, "z", axis=0, tiled=True)
    both, zero = lax.optimization_barrier((both, jnp.int32(0)))
    order = stage_order(rows, n_z, zero)
    beside = swap(both, "yl", 1)
    own = swap(both, "core", 1)
    beside, own, order = lax.optimization_barrier((beside, own, order))
    both = jnp.concatenate([both, beside, own, swap(beside, "core", 1)], axis=0)
    normed_all, grad_all = both[:, :width], both[:, width:]

    hidden = jnp.dot(normed_all, w_in, preferred_element_type=jnp.float32)
    gelu, derivative = gelu_both(hidden)
    activated = gelu.astype(jnp.bfloat16)
    act_grad = lax.dot_general(grad_all, w_out, contract_last, preferred_element_type=jnp.float32)
    hidden_grad = (act_grad * derivative).astype(jnp.bfloat16)
    ordered = jnp.dot(order, hidden_grad, preferred_element_type=jnp.float32).astype(jnp.bfloat16)
    half = ordered.shape[0] // 2
    send = lax.dot_general(
        ordered[half:], w_in, contract_last, preferred_element_type=jnp.float32
    ).astype(jnp.bfloat16)

    activated, hidden_grad, send = lax.optimization_barrier((activated, hidden_grad, send))
    part_in = lax.dot_general(
        hidden_grad, normed_all, contract_first, preferred_element_type=jnp.float32
    ).astype(jnp.bfloat16)
    part_out = lax.dot_general(
        activated, grad_all, contract_first, preferred_element_type=jnp.float32
    ).astype(jnp.bfloat16)
    parts = jnp.concatenate([part_in, part_out], axis=0).reshape(n_dp, -1, width)
    parts, ordered = lax.optimization_barrier((parts, ordered))
    parts = lax.all_to_all(parts, DP, 0, 0, tiled=True)

    keep = lax.dot_general(ordered[:half], w_in, contract_last, preferred_element_type=jnp.float32)
    sends = [send]
    for k, (axis, bits) in enumerate(STAGES):
        steps = (*bits, sum(bits))[: len(sends)]
        aways = [swap(send, axis, step) for send, step in zip(sends, steps)]
        if k == len(STAGES) - 1:
            break
        total = keep + sum(away.astype(jnp.float32) for away in aways)
        if k == 1:
            parts, _ = lax.optimization_barrier((parts, total))
            mine = (jnp.sum(parts.astype(jnp.float32), axis=0) / n_dp).astype(jnp.bfloat16)
            spread = jnp.broadcast_to(mine[None], (n_dp, *mine.shape))
        if k == 1:
            spread, total = lax.optimization_barrier((spread, total))
            spread = lax.all_to_all(spread, DP, 0, 0, tiled=True)
        size = total.shape[0] // 2 ** len(STAGES[k + 1][1])
        keep = total[:size]
        sends = [total[q : q + size].astype(jnp.bfloat16) for q in range(size, total.shape[0], size)]
    spread = spread.reshape(2, -1, width)
    grad_in = spread[0].T
    grad_out = spread[1]
    input_grad = pl.pallas_call(
        back_kernel,
        out_shape=jax.ShapeDtypeStruct(inputs.shape, jnp.bfloat16),
        cost_estimate=pl.CostEstimate(flops=0, bytes_accessed=0, transcendentals=0),
        name="norm_back",
    )(keep, normal, inverse, gain[None, :], cotangent, *aways)
    return (input_grad, grad_in, grad_out)


def solution(mesh):
    fine = Mesh(mesh.devices.reshape(4, 2, 2, 16, 2), AXES)
    rows, hidden_split = P(DP + MP, None), P(None, MP)
    in_specs = (rows, P(), hidden_split, P(MP, None), rows)
    out_specs = (rows, hidden_split, P(MP, None))
    return jax.shard_map(body, mesh=fine, in_specs=in_specs, out_specs=out_specs, check_vma=False)
```

```python
import math

import jax
import jax.numpy as jnp
from jax import lax
from jax.experimental import pallas as pl
from jax.sharding import Mesh, PartitionSpec as P

AXES = ("x", "yh", "yl", "z", "core")
DP = ("x", "yh")
MP = ("yl", "z", "core")
STAGES = (("core", (1,)), ("z", (1, 2,)), ("yl", (1,)), ("z", (4, 8,)))
contract_last = (((1,), (1,)), ((), ()))
contract_first = (((0,), (0,)), ((), ()))


def gelu_both(value):
    slope = math.sqrt(2.0 / math.pi)
    tangent = jnp.tanh(slope * (value + 0.044715 * value * value * value))
    gelu = 0.5 * value * (1.0 + tangent)
    derivative = 0.5 * (1.0 + tangent) + 0.5 * value * (1.0 - tangent * tangent) * slope * (
        1.0 + 3.0 * 0.044715 * value * value
    )
    return gelu, derivative


def swap(rows, axis, step):
    return lax.ppermute(rows, axis, [(at, at ^ step) for at in range(lax.axis_size(axis))])


def stage_order(rows, n_z, zero):
    at = lax.broadcasted_iota(jnp.int32, (4 * n_z * rows, 4 * n_z * rows), 0) + zero
    column = lax.broadcasted_iota(jnp.int32, at.shape, 1)
    old = at % rows
    far = jnp.zeros_like(at)
    block = at.shape[0]
    for axis, bits in STAGES:
        for step in reversed(bits):
            block //= 2
            bit = (at // block) % 2
            if axis == "z":
                far = far + bit * step
            else:
                old = old + bit * (n_z * rows * (2 if axis == "core" else 1))
    old = old + (far ^ lax.axis_index("z")) * rows
    return (old == column).astype(jnp.bfloat16)


def norm_kernel(inputs, gain, cotangent, joined, normal_out, inverse_out):
    width = inputs.shape[1]
    widened = inputs[...].astype(jnp.float32)
    centred = widened - jnp.mean(widened, axis=1, keepdims=True)
    variance = jnp.mean(centred * centred, axis=1, keepdims=True)
    inverse = 1.0 / jnp.sqrt(variance + 1e-06)
    normal = centred * inverse
    joined[:, :width] = (normal * gain[...]).astype(jnp.bfloat16)
    joined[:, width:] = cotangent[...]
    normal_out[...] = normal
    inverse_out[...] = jnp.broadcast_to(inverse, inverse_out.shape)


def join_normed(inputs, gain, cotangent):
    rows, width = inputs.shape
    return pl.pallas_call(
        norm_kernel,
        out_shape=(
            jax.ShapeDtypeStruct((rows, 2 * width), jnp.bfloat16),
            jax.ShapeDtypeStruct((rows, width), jnp.float32),
            jax.ShapeDtypeStruct((rows, 128), jnp.float32),
        ),
        name="norm",
    )(inputs, gain[None, :], cotangent)


def back_kernel(keep, normal, inverse, gain, cotangent, *rest):
    *aways, result = rest
    normal = normal[...]
    terms = keep[...]
    for away in aways:
        terms = terms + away[...].astype(jnp.float32)
    scaled = terms * gain[...]
    first_mean = jnp.mean(scaled, axis=1, keepdims=True)
    second_mean = jnp.mean(scaled * normal, axis=1, keepdims=True)
    change = (scaled - first_mean - normal * second_mean) * inverse[:, :1]
    result[...] = (cotangent[...].astype(jnp.float32) + change).astype(jnp.bfloat16)


def body(inputs, gain, w_in, w_out, cotangent):
    rows, width = inputs.shape
    n_dp = lax.axis_size(DP)
    n_z = lax.axis_size("z")
    joined, normal, inverse = join_normed(inputs, gain, cotangent)

    both = lax.all_gather(joined, "z", axis=0, tiled=True)
    both, zero = lax.optimization_barrier((both, jnp.int32(0)))
    order = stage_order(rows, n_z, zero)
    beside = swap(both, "yl", 1)
    own = swap(both, "core", 1)
    beside, own, order = lax.optimization_barrier((beside, own, order))
    both = jnp.concatenate([both, beside, own, swap(beside, "core", 1)], axis=0)
    normed_all, grad_all = both[:, :width], both[:, width:]

    hidden = jnp.dot(normed_all, w_in, preferred_element_type=jnp.float32)
    gelu, derivative = gelu_both(hidden)
    activated = gelu.astype(jnp.bfloat16)
    act_grad = lax.dot_general(grad_all, w_out, contract_last, preferred_element_type=jnp.float32)
    hidden_grad = (act_grad * derivative).astype(jnp.bfloat16)
    ordered = jnp.dot(order, hidden_grad, preferred_element_type=jnp.float32).astype(jnp.bfloat16)
    half = ordered.shape[0] // 2
    send = lax.dot_general(
        ordered[half:], w_in, contract_last, preferred_element_type=jnp.float32
    ).astype(jnp.bfloat16)

    activated, hidden_grad, send = lax.optimization_barrier((activated, hidden_grad, send))
    part_in = lax.dot_general(
        hidden_grad, normed_all, contract_first, preferred_element_type=jnp.float32
    ).astype(jnp.bfloat16)
    part_out = lax.dot_general(
        activated, grad_all, contract_first, preferred_element_type=jnp.float32
    ).astype(jnp.bfloat16)
    parts = jnp.concatenate([part_in, part_out], axis=0).reshape(n_dp, -1, width)
    parts, ordered = lax.optimization_barrier((parts, ordered))
    parts = lax.all_to_all(parts, DP, 0, 0, tiled=True)

    keep = lax.dot_general(ordered[:half], w_in, contract_last, preferred_element_type=jnp.float32)
    sends = [send]
    for k, (axis, bits) in enumerate(STAGES):
        steps = (*bits, sum(bits))[: len(sends)]
        aways = [swap(send, axis, step) for send, step in zip(sends, steps)]
        if k == len(STAGES) - 1:
            break
        total = keep + sum(away.astype(jnp.float32) for away in aways)
        if k == 2:
            parts, _ = lax.optimization_barrier((parts, total))
            mine = (jnp.sum(parts.astype(jnp.float32), axis=0) / n_dp).astype(jnp.bfloat16)
            spread = jnp.broadcast_to(mine[None], (n_dp, *mine.shape))
        if k == 2:
            spread, total = lax.optimization_barrier((spread, total))
            spread = lax.all_to_all(spread, DP, 0, 0, tiled=True)
        size = total.shape[0] // 2 ** len(STAGES[k + 1][1])
        keep = total[:size]
        sends = [total[q : q + size].astype(jnp.bfloat16) for q in range(size, total.shape[0], size)]
    spread = spread.reshape(2, -1, width)
    grad_in = spread[0].T
    grad_out = spread[1]
    input_grad = pl.pallas_call(
        back_kernel,
        out_shape=jax.ShapeDtypeStruct(inputs.shape, jnp.bfloat16),
        cost_estimate=pl.CostEstimate(flops=0, bytes_accessed=0, transcendentals=0),
        name="norm_back",
    )(keep, normal, inverse, gain[None, :], cotangent, *aways)
    return (input_grad, grad_in, grad_out)


def solution(mesh):
    fine = Mesh(mesh.devices.reshape(4, 2, 2, 16, 2), AXES)
    rows, hidden_split = P(DP + MP, None), P(None, MP)
    in_specs = (rows, P(), hidden_split, P(MP, None), rows)
    out_specs = (rows, hidden_split, P(MP, None))
    return jax.shard_map(body, mesh=fine, in_specs=in_specs, out_specs=out_specs, check_vma=False)
```

```python
import math

import jax
import jax.numpy as jnp
from jax import lax
from jax.experimental import pallas as pl
from jax.sharding import Mesh, PartitionSpec as P

AXES = ("x", "yh", "yl", "z", "core")
DP = ("x", "yh")
MP = ("yl", "z", "core")
STAGES = (("core", (1,)), ("z", (1, 2,)), ("yl", (1,)), ("z", (4, 8,)))
contract_last = (((1,), (1,)), ((), ()))
contract_first = (((0,), (0,)), ((), ()))


def gelu_both(value):
    slope = math.sqrt(2.0 / math.pi)
    tangent = jnp.tanh(slope * (value + 0.044715 * value * value * value))
    gelu = 0.5 * value * (1.0 + tangent)
    derivative = 0.5 * (1.0 + tangent) + 0.5 * value * (1.0 - tangent * tangent) * slope * (
        1.0 + 3.0 * 0.044715 * value * value
    )
    return gelu, derivative


def swap(rows, axis, step):
    return lax.ppermute(rows, axis, [(at, at ^ step) for at in range(lax.axis_size(axis))])


def mixed_rings(n_z):
    return [[2 * z + (z % 2 ^ core) for z in range(n_z)] for core in range(2)]


def stage_order(rows, n_z, zero):
    at = lax.broadcasted_iota(jnp.int32, (4 * n_z * rows, 4 * n_z * rows), 0) + zero
    column = lax.broadcasted_iota(jnp.int32, at.shape, 1)
    old = at % rows
    far = jnp.zeros_like(at)
    block = at.shape[0]
    for axis, bits in STAGES:
        for step in reversed(bits):
            block //= 2
            bit = (at // block) % 2
            if axis == "z":
                far = far + bit * step
            elif axis == "yl":
                old = old + bit * (n_z * rows)
            else:
                other = bit
    old = old + (other ^ far % 2) * (2 * n_z * rows)
    old = old + (far ^ lax.axis_index("z")) * rows
    return (old == column).astype(jnp.bfloat16)


def norm_kernel(inputs, gain, cotangent, joined, normal_out, inverse_out):
    width = inputs.shape[1]
    widened = inputs[...].astype(jnp.float32)
    centred = widened - jnp.mean(widened, axis=1, keepdims=True)
    variance = jnp.mean(centred * centred, axis=1, keepdims=True)
    inverse = 1.0 / jnp.sqrt(variance + 1e-06)
    normal = centred * inverse
    joined[:, :width] = (normal * gain[...]).astype(jnp.bfloat16)
    joined[:, width:] = cotangent[...]
    normal_out[...] = normal
    inverse_out[...] = jnp.broadcast_to(inverse, inverse_out.shape)


def join_normed(inputs, gain, cotangent):
    rows, width = inputs.shape
    return pl.pallas_call(
        norm_kernel,
        out_shape=(
            jax.ShapeDtypeStruct((rows, 2 * width), jnp.bfloat16),
            jax.ShapeDtypeStruct((rows, width), jnp.float32),
            jax.ShapeDtypeStruct((rows, 128), jnp.float32),
        ),
        name="norm",
    )(inputs, gain[None, :], cotangent)


def back_kernel(keep, normal, inverse, gain, cotangent, *rest):
    *aways, result = rest
    normal = normal[...]
    terms = keep[...]
    for away in aways:
        terms = terms + away[...].astype(jnp.float32)
    scaled = terms * gain[...]
    first_mean = jnp.mean(scaled, axis=1, keepdims=True)
    second_mean = jnp.mean(scaled * normal, axis=1, keepdims=True)
    change = (scaled - first_mean - normal * second_mean) * inverse[:, :1]
    result[...] = (cotangent[...].astype(jnp.float32) + change).astype(jnp.bfloat16)


def body(inputs, gain, w_in, w_out, cotangent):
    rows, width = inputs.shape
    n_dp = lax.axis_size(DP)
    n_z = lax.axis_size("z")
    joined, normal, inverse = join_normed(inputs, gain, cotangent)

    both = lax.all_gather(joined, ("z", "core"), axis_index_groups=mixed_rings(n_z), axis=0, tiled=True)
    both, zero = lax.optimization_barrier((both, jnp.int32(0)))
    order = stage_order(rows, n_z, zero)
    beside = swap(both, "yl", 1)
    own = swap(both, "core", 1)
    beside, own, order = lax.optimization_barrier((beside, own, order))
    both = jnp.concatenate([both, beside, own, swap(beside, "core", 1)], axis=0)
    normed_all, grad_all = both[:, :width], both[:, width:]

    hidden = jnp.dot(normed_all, w_in, preferred_element_type=jnp.float32)
    gelu, derivative = gelu_both(hidden)
    activated = gelu.astype(jnp.bfloat16)
    act_grad = lax.dot_general(grad_all, w_out, contract_last, preferred_element_type=jnp.float32)
    hidden_grad = (act_grad * derivative).astype(jnp.bfloat16)
    ordered = jnp.dot(order, hidden_grad, preferred_element_type=jnp.float32).astype(jnp.bfloat16)
    half = ordered.shape[0] // 2
    send = lax.dot_general(
        ordered[half:], w_in, contract_last, preferred_element_type=jnp.float32
    ).astype(jnp.bfloat16)

    activated, hidden_grad, send = lax.optimization_barrier((activated, hidden_grad, send))
    part_in = lax.dot_general(
        hidden_grad, normed_all, contract_first, preferred_element_type=jnp.float32
    ).astype(jnp.bfloat16)
    part_out = lax.dot_general(
        activated, grad_all, contract_first, preferred_element_type=jnp.float32
    ).astype(jnp.bfloat16)
    parts = jnp.concatenate([part_in, part_out], axis=0).reshape(n_dp, -1, width)
    parts, ordered = lax.optimization_barrier((parts, ordered))
    parts = lax.all_to_all(parts, DP, 0, 0, tiled=True)

    keep = lax.dot_general(ordered[:half], w_in, contract_last, preferred_element_type=jnp.float32)
    sends = [send]
    for k, (axis, bits) in enumerate(STAGES):
        steps = (*bits, sum(bits))[: len(sends)]
        aways = [swap(send, axis, step) for send, step in zip(sends, steps)]
        if k == len(STAGES) - 1:
            break
        total = keep + sum(away.astype(jnp.float32) for away in aways)
        if k == 2:
            parts, _ = lax.optimization_barrier((parts, total))
            mine = (jnp.sum(parts.astype(jnp.float32), axis=0) / n_dp).astype(jnp.bfloat16)
            spread = jnp.broadcast_to(mine[None], (n_dp, *mine.shape))
        if k == 2:
            spread, total = lax.optimization_barrier((spread, total))
            spread = lax.all_to_all(spread, DP, 0, 0, tiled=True)
        size = total.shape[0] // 2 ** len(STAGES[k + 1][1])
        keep = total[:size]
        sends = [total[q : q + size].astype(jnp.bfloat16) for q in range(size, total.shape[0], size)]
    spread = spread.reshape(2, -1, width)
    grad_in = spread[0].T
    grad_out = spread[1]
    input_grad = pl.pallas_call(
        back_kernel,
        out_shape=jax.ShapeDtypeStruct(inputs.shape, jnp.bfloat16),
        cost_estimate=pl.CostEstimate(flops=0, bytes_accessed=0, transcendentals=0),
        name="norm_back",
    )(keep, normal, inverse, gain[None, :], cotangent, *aways)
    return (input_grad, grad_in, grad_out)


def solution(mesh):
    fine = Mesh(mesh.devices.reshape(4, 2, 2, 16, 2), AXES)
    rows, hidden_split = P(DP + MP, None), P(None, MP)
    in_specs = (rows, P(), hidden_split, P(MP, None), rows)
    out_specs = (rows, hidden_split, P(MP, None))
    return jax.shard_map(body, mesh=fine, in_specs=in_specs, out_specs=out_specs, check_vma=False)
```

```python
import math

import jax
import jax.numpy as jnp
from jax import lax
from jax.experimental import pallas as pl
from jax.sharding import Mesh, PartitionSpec as P

AXES = ("x", "yh", "yl", "z", "core")
DP = ("x", "yh")
MP = ("yl", "z", "core")
STAGES = (("core", (1,)), ("z", (1, 2,)), ("yl", (1,)), ("z", (4, 8,)))
contract_last = (((1,), (1,)), ((), ()))
contract_first = (((0,), (0,)), ((), ()))


def gelu_both(value):
    slope = math.sqrt(2.0 / math.pi)
    tangent = jnp.tanh(slope * (value + 0.044715 * value * value * value))
    gelu = 0.5 * value * (1.0 + tangent)
    derivative = 0.5 * (1.0 + tangent) + 0.5 * value * (1.0 - tangent * tangent) * slope * (
        1.0 + 3.0 * 0.044715 * value * value
    )
    return gelu, derivative


def swap(rows, axis, step):
    return lax.ppermute(rows, axis, [(at, at ^ step) for at in range(lax.axis_size(axis))])


def stage_order(rows, n_z, zero):
    at = lax.broadcasted_iota(jnp.int32, (4 * n_z * rows, 4 * n_z * rows), 0) + zero
    column = lax.broadcasted_iota(jnp.int32, at.shape, 1)
    old = at % rows
    far = jnp.zeros_like(at)
    block = at.shape[0]
    for axis, bits in STAGES:
        for step in reversed(bits):
            block //= 2
            bit = (at // block) % 2
            if axis == "z":
                far = far + bit * step
            else:
                old = old + bit * (n_z * rows * (2 if axis == "core" else 1))
    old = old + (far ^ lax.axis_index("z")) * rows
    return (old == column).astype(jnp.bfloat16)


def norm_kernel(inputs, gain, cotangent, joined, normal_out, inverse_out):
    width = inputs.shape[1]
    widened = inputs[...].astype(jnp.float32)
    centred = widened - jnp.mean(widened, axis=1, keepdims=True)
    variance = jnp.mean(centred * centred, axis=1, keepdims=True)
    inverse = 1.0 / jnp.sqrt(variance + 1e-06)
    normal = centred * inverse
    joined[:, :width] = (normal * gain[...]).astype(jnp.bfloat16)
    joined[:, width:] = cotangent[...]
    normal_out[...] = normal
    inverse_out[...] = jnp.broadcast_to(inverse, inverse_out.shape)


def join_normed(inputs, gain, cotangent):
    rows, width = inputs.shape
    return pl.pallas_call(
        norm_kernel,
        out_shape=(
            jax.ShapeDtypeStruct((rows, 2 * width), jnp.bfloat16),
            jax.ShapeDtypeStruct((rows, width), jnp.float32),
            jax.ShapeDtypeStruct((rows, 128), jnp.float32),
        ),
        name="norm",
    )(inputs, gain[None, :], cotangent)


def back_kernel(keep, normal, inverse, gain, cotangent, *rest):
    *aways, result = rest
    normal = normal[...]
    terms = keep[...]
    for away in aways:
        terms = terms + away[...].astype(jnp.float32)
    scaled = terms * gain[...]
    first_mean = jnp.mean(scaled, axis=1, keepdims=True)
    second_mean = jnp.mean(scaled * normal, axis=1, keepdims=True)
    change = (scaled - first_mean - normal * second_mean) * inverse[:, :1]
    result[...] = (cotangent[...].astype(jnp.float32) + change).astype(jnp.bfloat16)


def body(inputs, gain, w_in, w_out, cotangent):
    rows, width = inputs.shape
    n_dp = lax.axis_size(DP)
    n_z = lax.axis_size("z")
    joined, normal, inverse = join_normed(inputs, gain, cotangent)

    both = lax.all_gather(joined, "z", axis=0, tiled=True)
    both, zero = lax.optimization_barrier((both, jnp.int32(0)))
    order = stage_order(rows, n_z, zero)
    beside = swap(both, "yl", 1)
    own = swap(both, "core", 1)
    beside, own, order = lax.optimization_barrier((beside, own, order))
    both = jnp.concatenate([both, beside, own, swap(beside, "core", 1)], axis=0)
    normed_all, grad_all = both[:, :width], both[:, width:]

    act_grad = lax.dot_general(grad_all, w_out, contract_last, preferred_element_type=jnp.float32)
    act_grad, w_in = lax.optimization_barrier((act_grad, w_in))
    hidden = jnp.dot(normed_all, w_in, preferred_element_type=jnp.float32)
    gelu, derivative = gelu_both(hidden)
    activated = gelu.astype(jnp.bfloat16)
    hidden_grad = (act_grad * derivative).astype(jnp.bfloat16)
    ordered = jnp.dot(order, hidden_grad, preferred_element_type=jnp.float32).astype(jnp.bfloat16)
    half = ordered.shape[0] // 2
    send = lax.dot_general(
        ordered[half:], w_in, contract_last, preferred_element_type=jnp.float32
    ).astype(jnp.bfloat16)

    activated, hidden_grad, send = lax.optimization_barrier((activated, hidden_grad, send))
    part_in = lax.dot_general(
        hidden_grad, normed_all, contract_first, preferred_element_type=jnp.float32
    ).astype(jnp.bfloat16)
    part_out = lax.dot_general(
        activated, grad_all, contract_first, preferred_element_type=jnp.float32
    ).astype(jnp.bfloat16)
    parts = jnp.concatenate([part_in, part_out], axis=0).reshape(n_dp, -1, width)
    parts, ordered = lax.optimization_barrier((parts, ordered))
    parts = lax.all_to_all(parts, DP, 0, 0, tiled=True)

    keep = lax.dot_general(ordered[:half], w_in, contract_last, preferred_element_type=jnp.float32)
    sends = [send]
    for k, (axis, bits) in enumerate(STAGES):
        steps = (*bits, sum(bits))[: len(sends)]
        aways = [swap(send, axis, step) for send, step in zip(sends, steps)]
        if k == len(STAGES) - 1:
            break
        total = keep + sum(away.astype(jnp.float32) for away in aways)
        if k == 2:
            parts, _ = lax.optimization_barrier((parts, total))
            mine = (jnp.sum(parts.astype(jnp.float32), axis=0) / n_dp).astype(jnp.bfloat16)
            spread = jnp.broadcast_to(mine[None], (n_dp, *mine.shape))
        if k == 2:
            spread, total = lax.optimization_barrier((spread, total))
            spread = lax.all_to_all(spread, DP, 0, 0, tiled=True)
        size = total.shape[0] // 2 ** len(STAGES[k + 1][1])
        keep = total[:size]
        sends = [total[q : q + size].astype(jnp.bfloat16) for q in range(size, total.shape[0], size)]
    spread = spread.reshape(2, -1, width)
    grad_in = spread[0].T
    grad_out = spread[1]
    input_grad = pl.pallas_call(
        back_kernel,
        out_shape=jax.ShapeDtypeStruct(inputs.shape, jnp.bfloat16),
        cost_estimate=pl.CostEstimate(flops=0, bytes_accessed=0, transcendentals=0),
        name="norm_back",
    )(keep, normal, inverse, gain[None, :], cotangent, *aways)
    return (input_grad, grad_in, grad_out)


def solution(mesh):
    fine = Mesh(mesh.devices.reshape(4, 2, 2, 16, 2), AXES)
    rows, hidden_split = P(DP + MP, None), P(None, MP)
    in_specs = (rows, P(), hidden_split, P(MP, None), rows)
    out_specs = (rows, hidden_split, P(MP, None))
    return jax.shard_map(body, mesh=fine, in_specs=in_specs, out_specs=out_specs, check_vma=False)
```

```python
import math

import jax
import jax.numpy as jnp
from jax import lax
from jax.experimental import pallas as pl
from jax.sharding import Mesh, PartitionSpec as P

AXES = ("x", "yh", "yl", "z", "core")
DP = ("x", "yh")
MP = ("yl", "z", "core")
STAGES = (("core", (1,)), ("z", (1, 2,)), ("yl", (1,)), ("z", (4, 8,)))
contract_last = (((1,), (1,)), ((), ()))
contract_first = (((0,), (0,)), ((), ()))


def gelu_both(value):
    slope = math.sqrt(2.0 / math.pi)
    tangent = jnp.tanh(slope * (value + 0.044715 * value * value * value))
    gelu = 0.5 * value * (1.0 + tangent)
    derivative = 0.5 * (1.0 + tangent) + 0.5 * value * (1.0 - tangent * tangent) * slope * (
        1.0 + 3.0 * 0.044715 * value * value
    )
    return gelu, derivative


def swap(rows, axis, step):
    return lax.ppermute(rows, axis, [(at, at ^ step) for at in range(lax.axis_size(axis))])


def stage_order(rows, n_z, zero):
    at = lax.broadcasted_iota(jnp.int32, (4 * n_z * rows, 4 * n_z * rows), 0) + zero
    column = lax.broadcasted_iota(jnp.int32, at.shape, 1)
    old = at % rows
    far = jnp.zeros_like(at)
    block = at.shape[0]
    for axis, bits in STAGES:
        for step in reversed(bits):
            block //= 2
            bit = (at // block) % 2
            if axis == "z":
                far = far + bit * step
            else:
                old = old + bit * (n_z * rows * (2 if axis == "core" else 1))
    old = old + (far ^ lax.axis_index("z")) * rows
    return (old == column).astype(jnp.bfloat16)


def norm_kernel(inputs, gain, cotangent, joined, normal_out, inverse_out):
    widened = inputs[...].astype(jnp.float32)
    centred = widened - jnp.mean(widened, axis=1, keepdims=True)
    variance = jnp.mean(centred * centred, axis=1, keepdims=True)
    inverse = 1.0 / jnp.sqrt(variance + 1e-06)
    normal = centred * inverse
    joined[0] = (normal * gain[...]).astype(jnp.bfloat16)
    joined[1] = cotangent[...]
    normal_out[...] = normal
    inverse_out[...] = jnp.broadcast_to(inverse, inverse_out.shape)


def join_normed(inputs, gain, cotangent):
    rows, width = inputs.shape
    return pl.pallas_call(
        norm_kernel,
        out_shape=(
            jax.ShapeDtypeStruct((2, rows, width), jnp.bfloat16),
            jax.ShapeDtypeStruct((rows, width), jnp.float32),
            jax.ShapeDtypeStruct((rows, 128), jnp.float32),
        ),
        name="norm",
    )(inputs, gain[None, :], cotangent)


def back_kernel(keep, normal, inverse, gain, cotangent, *rest):
    *aways, result = rest
    normal = normal[...]
    terms = keep[...]
    for away in aways:
        terms = terms + away[...].astype(jnp.float32)
    scaled = terms * gain[...]
    first_mean = jnp.mean(scaled, axis=1, keepdims=True)
    second_mean = jnp.mean(scaled * normal, axis=1, keepdims=True)
    change = (scaled - first_mean - normal * second_mean) * inverse[:, :1]
    result[...] = (cotangent[...].astype(jnp.float32) + change).astype(jnp.bfloat16)


def body(inputs, gain, w_in, w_out, cotangent):
    rows, width = inputs.shape
    n_dp = lax.axis_size(DP)
    n_z = lax.axis_size("z")
    joined, normal, inverse = join_normed(inputs, gain, cotangent)

    both = lax.all_gather(joined, "z").transpose(1, 0, 2, 3).reshape(2, -1, width)
    both, zero = lax.optimization_barrier((both, jnp.int32(0)))
    order = stage_order(rows, n_z, zero)
    beside = swap(both, "yl", 1)
    own = swap(both, "core", 1)
    beside, own, order = lax.optimization_barrier((beside, own, order))
    both = jnp.concatenate([both, beside, own, swap(beside, "core", 1)], axis=1)
    normed_all, grad_all = both[0], both[1]

    act_grad = lax.dot_general(grad_all, w_out, contract_last, preferred_element_type=jnp.float32)
    act_grad, w_in = lax.optimization_barrier((act_grad, w_in))
    hidden = jnp.dot(normed_all, w_in, preferred_element_type=jnp.float32)
    gelu, derivative = gelu_both(hidden)
    activated = gelu.astype(jnp.bfloat16)
    hidden_grad = (act_grad * derivative).astype(jnp.bfloat16)
    ordered = jnp.dot(order, hidden_grad, preferred_element_type=jnp.float32).astype(jnp.bfloat16)
    half = ordered.shape[0] // 2
    send = lax.dot_general(
        ordered[half:], w_in, contract_last, preferred_element_type=jnp.float32
    ).astype(jnp.bfloat16)

    activated, hidden_grad, send = lax.optimization_barrier((activated, hidden_grad, send))
    parts = lax.dot_general(
        jnp.stack([hidden_grad, activated]),
        both,
        (((1,), (1,)), ((0,), (0,))),
        preferred_element_type=jnp.float32,
    )
    parts = parts.astype(jnp.bfloat16).reshape(n_dp, -1, width)
    parts, ordered = lax.optimization_barrier((parts, ordered))
    parts = lax.all_to_all(parts, DP, 0, 0, tiled=True)

    keep = lax.dot_general(ordered[:half], w_in, contract_last, preferred_element_type=jnp.float32)
    sends = [send]
    for k, (axis, bits) in enumerate(STAGES):
        steps = (*bits, sum(bits))[: len(sends)]
        aways = [swap(send, axis, step) for send, step in zip(sends, steps)]
        if k == len(STAGES) - 1:
            break
        total = keep + sum(away.astype(jnp.float32) for away in aways)
        if k == 2:
            parts, _ = lax.optimization_barrier((parts, total))
            mine = (jnp.sum(parts.astype(jnp.float32), axis=0) / n_dp).astype(jnp.bfloat16)
            spread = jnp.broadcast_to(mine[None], (n_dp, *mine.shape))
        if k == 2:
            spread, total = lax.optimization_barrier((spread, total))
            spread = lax.all_to_all(spread, DP, 0, 0, tiled=True)
        size = total.shape[0] // 2 ** len(STAGES[k + 1][1])
        keep = total[:size]
        sends = [total[q : q + size].astype(jnp.bfloat16) for q in range(size, total.shape[0], size)]
    spread = spread.reshape(2, -1, width)
    grad_in = spread[0].T
    grad_out = spread[1]
    input_grad = pl.pallas_call(
        back_kernel,
        out_shape=jax.ShapeDtypeStruct(inputs.shape, jnp.bfloat16),
        cost_estimate=pl.CostEstimate(flops=0, bytes_accessed=0, transcendentals=0),
        name="norm_back",
    )(keep, normal, inverse, gain[None, :], cotangent, *aways)
    return (input_grad, grad_in, grad_out)


def solution(mesh):
    fine = Mesh(mesh.devices.reshape(4, 2, 2, 16, 2), AXES)
    rows, hidden_split = P(DP + MP, None), P(None, MP)
    in_specs = (rows, P(), hidden_split, P(MP, None), rows)
    out_specs = (rows, hidden_split, P(MP, None))
    return jax.shard_map(body, mesh=fine, in_specs=in_specs, out_specs=out_specs, check_vma=False)
```

```python
import math

import jax
import jax.numpy as jnp
from jax import lax
from jax.experimental import pallas as pl
from jax.sharding import Mesh, PartitionSpec as P

AXES = ("x", "yh", "yl", "z", "core")
DP = ("x", "yh")
MP = ("yl", "z", "core")
STAGES = (("core", (1,)), ("z", (1, 2,)), ("yl", (1,)), ("z", (4, 8,)))
contract_last = (((1,), (1,)), ((), ()))
contract_first = (((0,), (0,)), ((), ()))


def gelu_both(value):
    slope = math.sqrt(2.0 / math.pi)
    tangent = jnp.tanh(slope * (value + 0.044715 * value * value * value))
    gelu = 0.5 * value * (1.0 + tangent)
    derivative = 0.5 * (1.0 + tangent) + 0.5 * value * (1.0 - tangent * tangent) * slope * (
        1.0 + 3.0 * 0.044715 * value * value
    )
    return gelu, derivative


def swap(rows, axis, step):
    return lax.ppermute(rows, axis, [(at, at ^ step) for at in range(lax.axis_size(axis))])


def stage_order(rows, n_z, zero):
    at = lax.broadcasted_iota(jnp.int32, (4 * n_z * rows, 4 * n_z * rows), 0) + zero
    column = lax.broadcasted_iota(jnp.int32, at.shape, 1)
    old = at % rows
    far = jnp.zeros_like(at)
    block = at.shape[0]
    for axis, bits in STAGES:
        for step in reversed(bits):
            block //= 2
            bit = (at // block) % 2
            if axis == "z":
                far = far + bit * step
            else:
                old = old + bit * (n_z * rows * (2 if axis == "core" else 1))
    old = old + (far ^ lax.axis_index("z")) * rows
    return (old == column).astype(jnp.bfloat16)


def norm_kernel(inputs, gain, cotangent, joined, normal_out, inverse_out):
    widened = inputs[...].astype(jnp.float32)
    centred = widened - jnp.mean(widened, axis=1, keepdims=True)
    variance = jnp.mean(centred * centred, axis=1, keepdims=True)
    inverse = 1.0 / jnp.sqrt(variance + 1e-06)
    normal = centred * inverse
    joined[0] = (normal * gain[...]).astype(jnp.bfloat16)
    joined[1] = cotangent[...]
    normal_out[...] = normal
    inverse_out[...] = jnp.broadcast_to(inverse, inverse_out.shape)


def join_normed(inputs, gain, cotangent):
    rows, width = inputs.shape
    return pl.pallas_call(
        norm_kernel,
        out_shape=(
            jax.ShapeDtypeStruct((2, rows, width), jnp.bfloat16),
            jax.ShapeDtypeStruct((rows, width), jnp.float32),
            jax.ShapeDtypeStruct((rows, 128), jnp.float32),
        ),
        name="norm",
    )(inputs, gain[None, :], cotangent)


def back_kernel(keep, normal, inverse, gain, cotangent, *rest):
    *aways, result = rest
    normal = normal[...]
    terms = keep[...]
    for away in aways:
        terms = terms + away[...].astype(jnp.float32)
    scaled = terms * gain[...]
    first_mean = jnp.mean(scaled, axis=1, keepdims=True)
    second_mean = jnp.mean(scaled * normal, axis=1, keepdims=True)
    change = (scaled - first_mean - normal * second_mean) * inverse[:, :1]
    result[...] = (cotangent[...].astype(jnp.float32) + change).astype(jnp.bfloat16)


def body(inputs, gain, w_in, w_out, cotangent):
    rows, width = inputs.shape
    n_dp = lax.axis_size(DP)
    n_z = lax.axis_size("z")
    joined, normal, inverse = join_normed(inputs, gain, cotangent)

    both = lax.all_gather(joined, "z").transpose(1, 0, 2, 3).reshape(2, -1, width)
    both, zero = lax.optimization_barrier((both, jnp.int32(0)))
    order = stage_order(rows, n_z, zero)
    beside = swap(both, "yl", 1)
    own = swap(both, "core", 1)
    beside, own, order = lax.optimization_barrier((beside, own, order))
    both = jnp.concatenate([both, beside, own, swap(beside, "core", 1)], axis=1)
    normed_all, grad_all = both[0], both[1]

    act_grad = lax.dot_general(grad_all, w_out, contract_last, preferred_element_type=jnp.float32)
    act_grad, w_in = lax.optimization_barrier((act_grad, w_in))
    hidden = jnp.dot(normed_all, w_in, preferred_element_type=jnp.float32)
    gelu, derivative = gelu_both(hidden)
    activated = gelu.astype(jnp.bfloat16)
    hidden_grad = (act_grad * derivative).astype(jnp.bfloat16)
    ordered = jnp.dot(order, hidden_grad, preferred_element_type=jnp.float32).astype(jnp.bfloat16)
    half = ordered.shape[0] // 2
    send = lax.dot_general(
        ordered[half:], w_in, contract_last, preferred_element_type=jnp.float32
    ).astype(jnp.bfloat16)

    activated, hidden_grad, send = lax.optimization_barrier((activated, hidden_grad, send))
    parts = lax.dot_general(
        jnp.stack([hidden_grad, activated]),
        both,
        (((1,), (1,)), ((0,), (0,))),
        preferred_element_type=jnp.float32,
    )
    parts = parts.astype(jnp.bfloat16).reshape(n_dp, -1, width)
    parts, upper = lax.optimization_barrier((parts, ordered[:half]))
    parts = lax.all_to_all(parts, DP, 0, 0, tiled=True)

    keep = lax.dot_general(upper, w_in, contract_last, preferred_element_type=jnp.float32)
    sends = [send]
    for k, (axis, bits) in enumerate(STAGES):
        steps = (*bits, sum(bits))[: len(sends)]
        aways = [swap(send, axis, step) for send, step in zip(sends, steps)]
        if k == len(STAGES) - 1:
            break
        total = keep + sum(away.astype(jnp.float32) for away in aways)
        if k == 2:
            parts, _ = lax.optimization_barrier((parts, total))
            mine = (jnp.sum(parts.astype(jnp.float32), axis=0) / n_dp).astype(jnp.bfloat16)
            spread = jnp.broadcast_to(mine[None], (n_dp, *mine.shape))
        if k == 2:
            spread, total = lax.optimization_barrier((spread, total))
            spread = lax.all_to_all(spread, DP, 0, 0, tiled=True)
        size = total.shape[0] // 2 ** len(STAGES[k + 1][1])
        keep = total[:size]
        sends = [total[q : q + size].astype(jnp.bfloat16) for q in range(size, total.shape[0], size)]
    spread = spread.reshape(2, -1, width)
    grad_in = spread[0].T
    grad_out = spread[1]
    input_grad = pl.pallas_call(
        back_kernel,
        out_shape=jax.ShapeDtypeStruct(inputs.shape, jnp.bfloat16),
        cost_estimate=pl.CostEstimate(flops=0, bytes_accessed=0, transcendentals=0),
        name="norm_back",
    )(keep, normal, inverse, gain[None, :], cotangent, *aways)
    return (input_grad, grad_in, grad_out)


def solution(mesh):
    fine = Mesh(mesh.devices.reshape(4, 2, 2, 16, 2), AXES)
    rows, hidden_split = P(DP + MP, None), P(None, MP)
    in_specs = (rows, P(), hidden_split, P(MP, None), rows)
    out_specs = (rows, hidden_split, P(MP, None))
    return jax.shard_map(body, mesh=fine, in_specs=in_specs, out_specs=out_specs, check_vma=False)
```
